512 devices in a mesh: gx: 32 (over y_lo, z), gy: 16 (over y_hi, x, core).
Axes of the slice: x: 4, y: 8 (y_hi: 2, y_lo: 4; y = y_hi * 4 + y_lo), z: 8, core: 2. Of those that a mesh axis runs over, the one named last changes fastest.
Arguments:
- features: float32 [131072, 1024], P(('gx', 'gy')), may hold values from -6 to 6
- labels: int32 [512], replicated, may hold values from 0 to 1, as said below
- rounds: int32 [2], replicated, may hold values from 1 to 511, as said below
Outputs:
- feature_grad: float32 [131072, 1024], P(('gx', 'gy'))
The draws below stay inside these ranges and needn't reach their ends.
Inputs may be any that keep to these rules, and one draw needn't show every extreme that they name: Each of the two values labels some block. `rounds`: 2 different nonzero masks, one of which flips every bit of the block index.
All inputs are finite; a program needn't handle non-finite values.
Results may differ from the reference program's by a relative error of at most 0.0003.
Values sent between devices are 32-bit elements; how exact they have to be, the bound alone decides.
No kernel may reach another device: no remote copies, remote signals or barrier semaphores. Data moves between devices by JAX's collectives and lax.ppermute only.
A program may use at most 64 MiB of HBM per device.

```python
import jax
import jax.numpy as jnp
from jax import lax

D = 1024
ROWS_DEV = 256
ROUNDS = 2
BLOCKS = 512
ROWS_ALL = 131072


def draw_labels(key, part):
    key = jax.random.fold_in(key, 11)
    key_bits, key_order = jax.random.split(key)
    values = jax.random.randint(key_bits, (BLOCKS,), 0, 2).astype(jnp.int32)
    placing = jax.random.permutation(key_order, BLOCKS)
    values = values.at[placing[0]].set(1)
    values = values.at[placing[1]].set(0)
    return values.astype(jnp.int32)


def draw_rounds(key, part):
    key = jax.random.fold_in(key, 23)
    key_pick, key_place = jax.random.split(key)
    others = jax.random.permutation(key_pick, BLOCKS - 2)[:ROUNDS - 1] + 1
    full_flip = jnp.full((1,), BLOCKS - 1, dtype=jnp.int32)
    joined = jnp.concatenate([others.astype(jnp.int32), full_flip])
    placed = jax.random.permutation(key_place, joined)
    return placed.astype(jnp.int32)


def steps_of(stream_key, extent, cuts, low, top_value):
    def one(axis_at, parts):
        steps = jax.random.uniform(jax.random.fold_in(jax.random.fold_in(stream_key, 6), axis_at), (parts,), jnp.float32, low / len(cuts), top_value / len(cuts))
        return jnp.repeat(jnp.exp(steps), extent[axis_at] // parts).reshape((-1,) + (1,) * (len(extent) - axis_at - 1))

    gain = one(*cuts[0])
    for cut in cuts[1:]:
        gain = gain * one(*cut)
    return gain


def normal_values(stream_key, dims, scale, limit, cuts=(), kind=jnp.bfloat16):
    entries = scale * jax.random.normal(stream_key, dims, jnp.float32)
    if cuts:
        entries = entries * steps_of(stream_key, dims, cuts, -0.22, 0.18)
    return jnp.clip(entries, -limit, limit).astype(kind)


def setup_inputs(seed: int = 0) -> dict:
    arg_keys = jax.random.split(jax.random.key(seed), 4)
    return {
        "features": normal_values(arg_keys[0], (ROWS_ALL, D), 1.0, 6.0, ((0, 512),), jnp.float32),
        "labels": draw_labels(jax.random.fold_in(arg_keys[3], 71), 0),
        "rounds": draw_rounds(jax.random.fold_in(arg_keys[3], 71), 0),
    }


def pair_weight(label_own, label_other, real_rows, fake_rows, loss_scale):
    both_real = loss_scale / (real_rows * (real_rows - 1.0))
    both_fake = loss_scale / (fake_rows * (fake_rows - 1.0))
    mixed = -loss_scale / (real_rows * fake_rows)
    same = label_own == label_other
    return jnp.where(same, jnp.where(label_own == 1, both_real, both_fake), mixed)

def tile_grad(own_rows, partner, weight, skip_diag):
    root_width = jnp.sqrt(jnp.float32(D))
    scores = jnp.dot(own_rows, partner.T, precision=lax.Precision.HIGHEST) / root_width
    coefficient = weight * (6.0 / root_width) * (scores + 1.0) ** 2
    if skip_diag:
        coefficient = jnp.where(jnp.eye(ROWS_DEV, dtype=bool), jnp.float32(0.0), coefficient)
    return jnp.dot(coefficient, partner, precision=lax.Precision.HIGHEST)

def reference(features, labels, rounds):
    real_rows = jnp.float32(ROWS_DEV) * jnp.sum(labels).astype(jnp.float32)
    fake_rows = jnp.float32(ROWS_ALL) - real_rows
    loss_scale = float(ROWS_ALL) * float(ROWS_ALL) / 16.0

    def one_block(block_id):
        own_rows = lax.dynamic_slice_in_dim(features, (block_id * ROWS_DEV).astype(jnp.int32), ROWS_DEV, 0)
        label_own = labels[block_id]
        gradient = tile_grad(own_rows, own_rows, pair_weight(label_own, label_own, real_rows, fake_rows, loss_scale), True)
        for round_index in range(ROUNDS):
            partner_id = jnp.bitwise_xor(block_id, rounds[round_index]).astype(jnp.int32)
            partner = lax.dynamic_slice_in_dim(features, (partner_id * ROWS_DEV).astype(jnp.int32), ROWS_DEV, 0)
            weight = pair_weight(label_own, labels[partner_id], real_rows, fake_rows, loss_scale)
            gradient = gradient + tile_grad(own_rows, partner, weight, False)
        return gradient
    gradients = lax.map(one_block, jnp.arange(BLOCKS, dtype=jnp.int32))
    return gradients.reshape(ROWS_ALL, D)
```

```python
import functools
import math

import jax
import jax.numpy as jnp
from jax import lax
from jax.experimental import pallas as pl
from jax.experimental.pallas import tpu as pltpu
from jax.sharding import PartitionSpec as P

AXES = ("gx", "gy")
CORE, X0, X1, Y_HI, Z0, Z1, Z_HI, Y0, Y1 = (1 << place for place in range(9))
LIGHT = (X0, X1, Z0, Y0)
HEAVY = (Z1, Z_HI, Y1, Y_HI)
STRIP = 256


def halves(values):
    high = values.astype(jnp.bfloat16)
    return high, (values - high.astype(jnp.float32)).astype(jnp.bfloat16)


def product(left, right, contract):
    dims = (contract, ((), ()))
    dot = functools.partial(lax.dot_general, dimension_numbers=dims, preferred_element_type=jnp.float32)
    (left_high, left_low), (right_high, right_low) = halves(left), halves(right)
    return dot(left_low, right_high) + dot(left_high, right_low) + dot(left_high, right_high)


def tiles_kernel(blocks, kinds, own_id, rounds, labels, own, *refs):
    partners, out = refs[: len(kinds)], refs[-1]
    base = refs[len(kinds)] if len(refs) > len(kinds) + 1 else None
    row_count, width = own.shape
    marks = labels[...]
    place = lax.broadcasted_iota(jnp.int32, marks.shape, 0) * marks.shape[1] + lax.broadcasted_iota(
        jnp.int32, marks.shape, 1
    )

    def label_at(block):
        return jnp.sum(jnp.where(place == block, marks, 0))

    all_rows = row_count * blocks
    loss_scale = float(all_rows) * float(all_rows) / 16.0
    real_rows = jnp.float32(row_count) * jnp.sum(marks).astype(jnp.float32)
    fake_rows = jnp.float32(all_rows) - real_rows
    block = own_id[0]
    label_own = label_at(block)
    full = blocks - 1
    masks = {"own": 0, "flip": full, "pick": rounds[0] ^ rounds[1] ^ full}
    root_width = math.sqrt(width)
    for index, kind in enumerate(kinds):
        partner = partners[index]
        label_other = label_at(block ^ masks[kind])
        both_real = loss_scale / (real_rows * (real_rows - 1.0))
        both_fake = loss_scale / (fake_rows * (fake_rows - 1.0))
        mixed = -loss_scale / (real_rows * fake_rows)
        weight = jnp.where(label_own == label_other, jnp.where(label_own == 1, both_real, both_fake), mixed)

        def add_scores(step, scores):
            strip = pl.ds(pl.multiple_of(step * STRIP, STRIP), STRIP)
            return scores + product(own[:, strip], partner[:, strip], ((1,), (1,)))

        scores = lax.fori_loop(0, width // STRIP, add_scores, jnp.zeros((row_count, row_count), jnp.float32))
        scores = scores * (1.0 / root_width) + 1.0
        coefficient = (weight * (6.0 / root_width)) * (scores * scores)
        if kind == "own":
            rows = lax.broadcasted_iota(jnp.int32, coefficient.shape, 0)
            columns = lax.broadcasted_iota(jnp.int32, coefficient.shape, 1)
            coefficient = jnp.where(rows == columns, 0.0, coefficient)
        before = base if index == 0 else out

        def add_gradient(step, carry):
            strip = pl.ds(pl.multiple_of(step * STRIP, STRIP), STRIP)
            part = product(coefficient, partner[:, strip], ((1,), (0,)))
            out[:, strip] = part if before is None else before[:, strip] + part
            return carry

        lax.fori_loop(0, width // STRIP, add_gradient, 0)


def add_tiles(blocks, kinds, own_id, rounds, labels, own, partners, base=None):
    row_count, width = own.shape
    scalars = [pl.BlockSpec(memory_space=pltpu.SMEM)] * 2
    arrays = [labels, own, *partners] + ([] if base is None else [base])
    flops = 4 * len(kinds) * row_count * row_count * width
    return pl.pallas_call(
        functools.partial(tiles_kernel, blocks, kinds),
        out_shape=jax.ShapeDtypeStruct(own.shape, jnp.float32),
        in_specs=scalars + [pl.BlockSpec(memory_space=pltpu.VMEM)] * len(arrays),
        out_specs=pl.BlockSpec(memory_space=pltpu.VMEM),
        compiler_params=pltpu.CompilerParams(vmem_limit_bytes=32 << 20),
        cost_estimate=pl.CostEstimate(
            flops=3 * flops, bytes_accessed=4 * row_count * width * len(arrays), transcendentals=0
        ),
    )(own_id, rounds, *arrays)


def flip(block, mask):
    count = lax.axis_size("gx") * lax.axis_size("gy")
    return lax.ppermute(block, AXES, [(source, source ^ mask) for source in range(count)])


def flip_by(block, mask, bits):
    choice = jnp.int32(0)
    for place, bit in enumerate(bits):
        choice = choice | (((mask & bit) != 0).astype(jnp.int32) << place)
    masks = [sum(bit for place, bit in enumerate(bits) if pick >> place & 1) for pick in range(1 << len(bits))]
    branches = [(lambda rows, m=m: flip(rows, m) if m else rows) for m in masks]
    return lax.switch(choice, branches, block)


def on_device(features, labels, rounds):
    blocks = lax.axis_size("gx") * lax.axis_size("gy")
    full = blocks - 1
    own_block = lax.axis_index("gx") * lax.axis_size("gy") + lax.axis_index("gy")
    own_id = own_block.astype(jnp.int32).reshape(1)
    labels = labels.reshape(-1, 128)
    mask = rounds[0] ^ rounds[1] ^ full
    far = flip(features, full)
    sibling = flip(features, CORE)
    gradient = add_tiles(blocks, ("own",), own_id, rounds, labels, features, (features,))
    near = jnp.where((mask & CORE) != 0, sibling, features)
    near = flip_by(near, mask, LIGHT)
    near = flip_by(near, mask, HEAVY)
    return add_tiles(blocks, ("flip", "pick"), own_id, rounds, labels, features, (far, near), gradient)


def solution(mesh):
    in_specs = (P(("gx", "gy"), None), P(), P())
    out_specs = P(("gx", "gy"), None)
    return jax.shard_map(
        on_device, mesh=mesh, in_specs=in_specs, out_specs=out_specs, check_vma=False
    )
```

```python
import functools
import math

import jax
import jax.numpy as jnp
from jax import lax
from jax.experimental import pallas as pl
from jax.experimental.pallas import tpu as pltpu
from jax.sharding import PartitionSpec as P

AXES = ("gx", "gy")
CORE, X0, X1, Y_HI, Z0, Z1, Z_HI, Y0, Y1 = (1 << place for place in range(9))
def halves(values):
    high = values.astype(jnp.bfloat16)
    return high, (values - high.astype(jnp.float32)).astype(jnp.bfloat16)


def dot(left, right, contract):
    return lax.dot_general(left, right, (contract, ((), ())), preferred_element_type=jnp.float32)


def product(left_pair, right_high, right_low, contract):
    rows = left_pair.shape[0] // 2
    both = dot(left_pair, right_high, contract)
    return (both[rows:] + dot(left_pair[:rows], right_low, contract)) + both[:rows]


def tiles_kernel(blocks, kinds, parts, own_id, rounds, labels, own, *refs):
    partners, rest = refs[: sum(parts)], refs[sum(parts) :]
    base = rest[0] if len(rest) == 6 else None
    out, own_pair, high, low, landing = rest[-5:]
    row_count, width = own.shape
    marks = labels[...]
    place = lax.broadcasted_iota(jnp.int32, marks.shape, 0) * marks.shape[1] + lax.broadcasted_iota(
        jnp.int32, marks.shape, 1
    )

    def label_at(block):
        return jnp.sum(jnp.where(place == block, marks, 0))

    all_rows = row_count * blocks
    loss_scale = float(all_rows) * float(all_rows) / 16.0
    real_rows = jnp.float32(row_count) * jnp.sum(marks).astype(jnp.float32)
    fake_rows = jnp.float32(all_rows) - real_rows
    both_real = loss_scale / (real_rows * (real_rows - 1.0))
    both_fake = loss_scale / (fake_rows * (fake_rows - 1.0))
    mixed = -loss_scale / (real_rows * fake_rows)
    block = own_id[0]
    label_own = label_at(block)
    full = blocks - 1
    masks = {"own": 0, "flip": full, "pick": rounds[0] ^ rounds[1] ^ full}
    root_width = math.sqrt(width)
    own_pair[:row_count, :], own_pair[row_count:, :] = halves(own[...])
    total = None if base is None else base[...]
    first = 0
    for kind, count in zip(kinds, parts):
        rows = 0
        for piece in partners[first : first + count]:
            here = slice(rows, rows + piece.shape[0])
            high[here, :], low[here, :] = halves(piece[...])
            rows += piece.shape[0]
        first += count
        weight = jnp.where(
            label_own == label_at(block ^ masks[kind]), jnp.where(label_own == 1, both_real, both_fake), mixed
        )
        right_high, right_low = high[:rows, :], low[:rows, :]
        scores = product(own_pair[...], right_high, right_low, ((1,), (1,))) * (1.0 / root_width) + 1.0
        coefficient = (weight * (6.0 / root_width)) * (scores * scores)
        if kind == "own":
            down = lax.broadcasted_iota(jnp.int32, coefficient.shape, 0)
            across = lax.broadcasted_iota(jnp.int32, coefficient.shape, 1)
            coefficient = jnp.where(down == across, 0.0, coefficient)
        pair = jnp.concatenate(halves(coefficient), axis=0)
        part = product(pair, right_high, right_low, ((1,), (0,)))
        total = part if total is None else total + part
        out[...] = total
        total = out[...]


def add_tiles(blocks, tiles, own_id, rounds, labels, own, base=None):
    row_count, width = own.shape
    scalar, held = pl.BlockSpec(memory_space=pltpu.SMEM), pl.BlockSpec(memory_space=pltpu.VMEM)
    kinds, parts = tuple(kind for kind, _ in tiles), tuple(len(pieces) for _, pieces in tiles)
    arrays = [labels, own] + [piece for _, pieces in tiles for piece in pieces] + ([] if base is None else [base])
    flops = 4 * len(kinds) * row_count * row_count * width
    return pl.pallas_call(
        functools.partial(tiles_kernel, blocks, kinds, parts),
        out_shape=jax.ShapeDtypeStruct(own.shape, jnp.float32),
        in_specs=[scalar, scalar] + [held] * len(arrays),
        out_specs=held,
        scratch_shapes=[
            pltpu.VMEM((2 * row_count, width), jnp.bfloat16),
            pltpu.VMEM((row_count, width), jnp.bfloat16),
            pltpu.VMEM((row_count, width), jnp.bfloat16),
            pltpu.VMEM((8, 128), jnp.float32),
        ],
        compiler_params=pltpu.CompilerParams(vmem_limit_bytes=32 << 20),
        cost_estimate=pl.CostEstimate(
            flops=3 * flops, bytes_accessed=4 * row_count * width * len(arrays), transcendentals=0
        ),
    )(own_id, rounds, *arrays)


def flip(block, mask):
    count = lax.axis_size("gx") * lax.axis_size("gy")
    return lax.ppermute(block, AXES, [(source, source ^ mask) for source in range(count)]) if mask else block


def subsets(bits):
    return [sum(bit for place, bit in enumerate(bits) if pick >> place & 1) for pick in range(1 << len(bits))]


def packed(flags):
    return sum(flag.astype(jnp.int32) << place for place, flag in enumerate(flags))


def on_device(features, labels, rounds):
    blocks = lax.axis_size("gx") * lax.axis_size("gy")
    full = blocks - 1
    own_block = lax.axis_index("gx") * lax.axis_size("gy") + lax.axis_index("gy")
    own_id = own_block.astype(jnp.int32).reshape(1)
    labels = labels.reshape(-1, 128)
    mask = rounds[0] ^ rounds[1] ^ full
    bit = {place: (mask & place) != 0 for place in (CORE, X0, X1, Y_HI, Z0, Z1, Z_HI, Y0, Y1)}
    half = features.shape[0] // 2
    top, bottom = features[:half], features[half:]

    inner = packed([bit[Y0] ^ bit[Y_HI], bit[Y1] ^ bit[Y_HI], bit[Z0] ^ bit[Z_HI], bit[Z1] ^ bit[Z_HI]])
    inner_moves = [functools.partial(flip, mask=move) for move in subsets((Y0, Y1, Z0, Z1))]

    far_bottom = flip(bottom, full)
    top_moved = lax.switch(inner, inner_moves, top)
    top_later, top_moved = lax.optimization_barrier((top, top_moved))
    far_top = flip(top_later, full)
    bottom_moved = lax.switch(inner, inner_moves, far_bottom)

    cross = bit[Y_HI]
    stays, crosses = jnp.where(cross, bottom_moved, top_moved), jnp.where(cross, top_moved, bottom_moved)
    along = (X0, X1, Z0 | Z1 | Z_HI)
    outer = packed([bit[place] ^ cross for place in (X0, X1, Z_HI)])
    rest = Y0 | Y1 | Y_HI | sum(along)
    outer_moves = [
        (lambda pair, move=move: (flip(pair[0], move), flip(pair[1], move ^ rest))) for move in subsets(along)
    ]
    stays, crosses = lax.switch(outer, outer_moves, (stays, crosses))

    swap = bit[CORE] ^ cross
    ready, sibling = jnp.where(swap, crosses, stays), jnp.where(swap, stays, crosses)
    swapped = flip(sibling, CORE)
    tiles = [("own", (features,)), ("flip", (far_top, far_bottom)), ("pick", (ready,))]
    gradient = add_tiles(blocks, tiles, own_id, rounds, labels, features)
    return add_tiles(blocks, [("pick", (swapped,))], own_id, rounds, labels, features, gradient)


def solution(mesh):
    in_specs = (P(("gx", "gy"), None), P(), P())
    out_specs = P(("gx", "gy"), None)
    return jax.shard_map(
        on_device, mesh=mesh, in_specs=in_specs, out_specs=out_specs, check_vma=False
    )
```

```python
import functools
import math

import jax
import jax.numpy as jnp
from jax import lax
from jax.experimental import pallas as pl
from jax.experimental.pallas import tpu as pltpu
from jax.sharding import PartitionSpec as P

AXES = ("gx", "gy")
CORE, X0, X1, Y_HI, Z0, Z1, Z_HI, Y0, Y1 = (1 << place for place in range(9))
def halves(values):
    high = values.astype(jnp.bfloat16)
    return high, (values - high.astype(jnp.float32)).astype(jnp.bfloat16)


def dot(left, right, contract):
    return lax.dot_general(left, right, (contract, ((), ())), preferred_element_type=jnp.float32)


def product(left_pair, right_high, right_low, contract):
    rows = left_pair.shape[0] // 2
    both = dot(left_pair, right_high, contract)
    return (both[rows:] + dot(left_pair[:rows], right_low, contract)) + both[:rows]


def tiles_kernel(blocks, kinds, parts, choices, own_id, rounds, labels, own, *refs):
    partners, chances, rest = refs[: sum(parts)], refs[sum(parts) : sum(parts) + choices], refs[sum(parts) + choices :]
    base = rest[0] if len(rest) == 7 else None
    out, own_pair, high, low, landing, sem = rest[-6:]
    row_count, width = own.shape
    if choices:
        second = swaps(rounds[0] ^ rounds[1] ^ (blocks - 1))
        for index, chance in enumerate(chances):

            @pl.when(second == (index == 1))
            def _():
                pltpu.make_async_copy(chance, landing, sem).start()

    marks = labels[...]
    place = lax.broadcasted_iota(jnp.int32, marks.shape, 0) * marks.shape[1] + lax.broadcasted_iota(
        jnp.int32, marks.shape, 1
    )

    def label_at(block):
        return jnp.sum(jnp.where(place == block, marks, 0))

    all_rows = row_count * blocks
    loss_scale = float(all_rows) * float(all_rows) / 16.0
    real_rows = jnp.float32(row_count) * jnp.sum(marks).astype(jnp.float32)
    fake_rows = jnp.float32(all_rows) - real_rows
    both_real = loss_scale / (real_rows * (real_rows - 1.0))
    both_fake = loss_scale / (fake_rows * (fake_rows - 1.0))
    mixed = -loss_scale / (real_rows * fake_rows)
    block = own_id[0]
    label_own = label_at(block)
    full = blocks - 1
    masks = {"own": 0, "flip": full, "pick": rounds[0] ^ rounds[1] ^ full}
    root_width = math.sqrt(width)
    own_pair[:row_count, :], own_pair[row_count:, :] = halves(own[...])
    total = None if base is None else base[...]
    pieces = list(partners)
    first = 0
    for kind, count in zip(kinds, parts):
        rows = 0
        if choices and kind == kinds[-1]:
            pltpu.make_async_copy(chances[0], landing, sem).wait()
            pieces, count = pieces + [landing], count + 1
        for piece in pieces[first : first + count]:
            here = slice(rows, rows + piece.shape[0])
            high[here, :], low[here, :] = halves(piece[...])
            rows += piece.shape[0]
        first += count
        weight = jnp.where(
            label_own == label_at(block ^ masks[kind]), jnp.where(label_own == 1, both_real, both_fake), mixed
        )
        right_high, right_low = high[:rows, :], low[:rows, :]
        scores = product(own_pair[...], right_high, right_low, ((1,), (1,))) * (1.0 / root_width) + 1.0
        coefficient = (weight * (6.0 / root_width)) * (scores * scores)
        if kind == "own":
            down = lax.broadcasted_iota(jnp.int32, coefficient.shape, 0)
            across = lax.broadcasted_iota(jnp.int32, coefficient.shape, 1)
            coefficient = jnp.where(down == across, 0.0, coefficient)
        pair = jnp.concatenate(halves(coefficient), axis=0)
        part = product(pair, right_high, right_low, ((1,), (0,)))
        total = part if total is None else total + part
        out[...] = total
        total = out[...]


def swaps(mask):
    return ((mask & CORE) != 0) != ((mask & Y_HI) != 0)


def add_tiles(blocks, tiles, own_id, rounds, labels, own, base=None, choices=()):
    row_count, width = own.shape
    scalar, held = pl.BlockSpec(memory_space=pltpu.SMEM), pl.BlockSpec(memory_space=pltpu.VMEM)
    kinds, parts = tuple(kind for kind, _ in tiles), tuple(len(pieces) for _, pieces in tiles)
    pieces = [piece for _, some in tiles for piece in some]
    arrays = [labels, own, *pieces, *choices] + ([] if base is None else [base])
    specs = [held] * (2 + len(pieces)) + [pl.BlockSpec(memory_space=pl.ANY)] * len(choices) + [held] * (base is not None)
    flops = 4 * len(kinds) * row_count * row_count * width
    return pl.pallas_call(
        functools.partial(tiles_kernel, blocks, kinds, parts, len(choices)),
        out_shape=jax.ShapeDtypeStruct(own.shape, jnp.float32),
        in_specs=[scalar, scalar] + specs,
        out_specs=held,
        scratch_shapes=[
            pltpu.VMEM((2 * row_count, width), jnp.bfloat16),
            pltpu.VMEM((row_count, width), jnp.bfloat16),
            pltpu.VMEM((row_count, width), jnp.bfloat16),
            pltpu.VMEM((row_count // 2, width), jnp.float32),
            pltpu.SemaphoreType.DMA,
        ],
        compiler_params=pltpu.CompilerParams(vmem_limit_bytes=32 << 20),
        cost_estimate=pl.CostEstimate(
            flops=3 * flops, bytes_accessed=4 * row_count * width * len(arrays), transcendentals=0
        ),
    )(own_id, rounds, *arrays)


def flip(block, mask):
    count = lax.axis_size("gx") * lax.axis_size("gy")
    return lax.ppermute(block, AXES, [(source, source ^ mask) for source in range(count)]) if mask else block


def subsets(bits):
    return [sum(bit for place, bit in enumerate(bits) if pick >> place & 1) for pick in range(1 << len(bits))]


def packed(flags):
    return sum(flag.astype(jnp.int32) << place for place, flag in enumerate(flags))


def on_device(features, labels, rounds):
    blocks = lax.axis_size("gx") * lax.axis_size("gy")
    full = blocks - 1
    own_block = lax.axis_index("gx") * lax.axis_size("gy") + lax.axis_index("gy")
    own_id = own_block.astype(jnp.int32).reshape(1)
    labels = labels.reshape(-1, 128)
    mask = rounds[0] ^ rounds[1] ^ full
    bit = {place: (mask & place) != 0 for place in (CORE, X0, X1, Y_HI, Z0, Z1, Z_HI, Y0, Y1)}
    half = features.shape[0] // 2
    top, bottom = features[:half], features[half:]

    inner = packed([bit[Y0] ^ bit[Y_HI], bit[Y1] ^ bit[Y_HI], bit[Z0] ^ bit[Z_HI], bit[Z1] ^ bit[Z_HI]])
    inner_moves = [functools.partial(flip, mask=move) for move in subsets((Y0, Y1, Z0, Z1))]

    far_bottom = flip(bottom, full)
    top_moved = lax.switch(inner, inner_moves, top)
    top_later, top_moved = lax.optimization_barrier((top, top_moved))
    far_top = flip(top_later, full)
    bottom_moved = lax.switch(inner, inner_moves, far_bottom)

    cross = bit[Y_HI]
    stays, crosses = jnp.where(cross, bottom_moved, top_moved), jnp.where(cross, top_moved, bottom_moved)
    along = (X0, X1, Z0 | Z1 | Z_HI)
    outer = packed([bit[place] ^ cross for place in (X0, X1, Z_HI)])
    rest = Y0 | Y1 | Y_HI | sum(along)
    outer_moves = [
        (lambda pair, move=move: (flip(pair[0], move ^ rest), flip(pair[1], move))) for move in subsets(along)
    ]
    crosses, stays = lax.switch(outer, outer_moves, (crosses, stays))

    sibling = jnp.where(swaps(mask), stays, crosses)
    swapped = flip(sibling, CORE)
    tiles = [("own", (features,)), ("flip", (far_top, far_bottom))]
    gradient = add_tiles(blocks, tiles, own_id, rounds, labels, features)
    tiles = [("pick", (swapped,))]
    return add_tiles(blocks, tiles, own_id, rounds, labels, features, gradient, (stays, crosses))


def solution(mesh):
    in_specs = (P(("gx", "gy"), None), P(), P())
    out_specs = P(("gx", "gy"), None)
    return jax.shard_map(
        on_device, mesh=mesh, in_specs=in_specs, out_specs=out_specs, check_vma=False
    )
```

```python
import functools
import math

import jax
import jax.numpy as jnp
from jax import lax
from jax.experimental import pallas as pl
from jax.experimental.pallas import tpu as pltpu
from jax.sharding import PartitionSpec as P

AXES = ("gx", "gy")
CORE, X0, X1, Y_HI, Z0, Z1, Z_HI, Y0, Y1 = (1 << place for place in range(9))
def halves(values):
    high = values.astype(jnp.bfloat16)
    return high, (values - high.astype(jnp.float32)).astype(jnp.bfloat16)


def dot(left, right, contract):
    return lax.dot_general(left, right, (contract, ((), ())), preferred_element_type=jnp.float32)


def product(left_pair, right_high, right_low, contract):
    rows = left_pair.shape[0] // 2
    both = dot(left_pair, right_high, contract)
    return (both[rows:] + dot(left_pair[:rows], right_low, contract)) + both[:rows]


def tiles_kernel(blocks, kinds, parts, choices, own_id, rounds, labels, own, *refs):
    partners, chances, rest = refs[: sum(parts)], refs[sum(parts) : sum(parts) + choices], refs[sum(parts) + choices :]
    base = rest[0] if len(rest) == 7 else None
    out, own_pair, high, low, landing, sem = rest[-6:]
    row_count, width = own.shape
    if choices:
        second = swaps(rounds[0] ^ rounds[1] ^ (blocks - 1))
        for index, chance in enumerate(chances):

            @pl.when(second == (index == 1))
            def _():
                pltpu.make_async_copy(chance, landing, sem).start()

    marks = labels[...]
    place = lax.broadcasted_iota(jnp.int32, marks.shape, 0) * marks.shape[1] + lax.broadcasted_iota(
        jnp.int32, marks.shape, 1
    )

    def label_at(block):
        return jnp.sum(jnp.where(place == block, marks, 0))

    all_rows = row_count * blocks
    loss_scale = float(all_rows) * float(all_rows) / 16.0
    real_rows = jnp.float32(row_count) * jnp.sum(marks).astype(jnp.float32)
    fake_rows = jnp.float32(all_rows) - real_rows
    both_real = loss_scale / (real_rows * (real_rows - 1.0))
    both_fake = loss_scale / (fake_rows * (fake_rows - 1.0))
    mixed = -loss_scale / (real_rows * fake_rows)
    block = own_id[0]
    label_own = label_at(block)
    full = blocks - 1
    masks = {"own": 0, "flip": full, "pick": rounds[0] ^ rounds[1] ^ full}
    root_width = math.sqrt(width)
    own_pair[:row_count, :], own_pair[row_count:, :] = halves(own[...])
    total = None if base is None else base[...]
    pieces = list(partners)
    first = 0
    for kind, count in zip(kinds, parts):
        rows = 0
        if choices and kind == kinds[-1]:
            pltpu.make_async_copy(chances[0], landing, sem).wait()
            pieces, count = pieces + [landing], count + 1
        for piece in pieces[first : first + count]:
            here = slice(rows, rows + piece.shape[0])
            high[here, :], low[here, :] = halves(piece[...])
            rows += piece.shape[0]
        first += count
        weight = jnp.where(
            label_own == label_at(block ^ masks[kind]), jnp.where(label_own == 1, both_real, both_fake), mixed
        )
        right_high, right_low = high[:rows, :], low[:rows, :]
        scores = product(own_pair[...], right_high, right_low, ((1,), (1,))) * (1.0 / root_width) + 1.0
        coefficient = (weight * (6.0 / root_width)) * (scores * scores)
        if kind == "own":
            down = lax.broadcasted_iota(jnp.int32, coefficient.shape, 0)
            across = lax.broadcasted_iota(jnp.int32, coefficient.shape, 1)
            coefficient = jnp.where(down == across, 0.0, coefficient)
        pair = jnp.concatenate(halves(coefficient), axis=0)
        part = product(pair, right_high, right_low, ((1,), (0,)))
        total = part if total is None else total + part
        out[...] = total
        total = out[...]


def swaps(mask):
    return ((mask & CORE) != 0) != ((mask & Y_HI) != 0)


def add_tiles(blocks, tiles, own_id, rounds, labels, own, base=None, choices=()):
    row_count, width = own.shape
    scalar, held = pl.BlockSpec(memory_space=pltpu.SMEM), pl.BlockSpec(memory_space=pltpu.VMEM)
    kinds, parts = tuple(kind for kind, _ in tiles), tuple(len(pieces) for _, pieces in tiles)
    pieces = [piece for _, some in tiles for piece in some]
    arrays = [labels, own, *pieces, *choices] + ([] if base is None else [base])
    specs = [held] * (2 + len(pieces)) + [pl.BlockSpec(memory_space=pl.ANY)] * len(choices) + [held] * (base is not None)
    flops = 4 * len(kinds) * row_count * row_count * width
    return pl.pallas_call(
        functools.partial(tiles_kernel, blocks, kinds, parts, len(choices)),
        out_shape=jax.ShapeDtypeStruct(own.shape, jnp.float32),
        in_specs=[scalar, scalar] + specs,
        out_specs=held,
        scratch_shapes=[
            pltpu.VMEM((2 * row_count, width), jnp.bfloat16),
            pltpu.VMEM((row_count, width), jnp.bfloat16),
            pltpu.VMEM((row_count, width), jnp.bfloat16),
            pltpu.VMEM((row_count // 2, width), jnp.float32),
            pltpu.SemaphoreType.DMA,
        ],
        compiler_params=pltpu.CompilerParams(vmem_limit_bytes=32 << 20),
        cost_estimate=pl.CostEstimate(
            flops=3 * flops, bytes_accessed=4 * row_count * width * len(arrays), transcendentals=0
        ),
    )(own_id, rounds, *arrays)


def flip(block, mask):
    count = lax.axis_size("gx") * lax.axis_size("gy")
    return lax.ppermute(block, AXES, [(source, source ^ mask) for source in range(count)]) if mask else block


def subsets(bits):
    return [sum(bit for place, bit in enumerate(bits) if pick >> place & 1) for pick in range(1 << len(bits))]


def packed(flags):
    return sum(flag.astype(jnp.int32) << place for place, flag in enumerate(flags))


def on_device(features, labels, rounds):
    blocks = lax.axis_size("gx") * lax.axis_size("gy")
    full = blocks - 1
    own_block = lax.axis_index("gx") * lax.axis_size("gy") + lax.axis_index("gy")
    own_id = own_block.astype(jnp.int32).reshape(1)
    labels = labels.reshape(-1, 128)
    mask = rounds[0] ^ rounds[1] ^ full
    bit = {place: (mask & place) != 0 for place in (CORE, X0, X1, Y_HI, Z0, Z1, Z_HI, Y0, Y1)}
    half = features.shape[0] // 2
    top = features[:half]

    inner = packed([bit[Y0] ^ bit[Y_HI], bit[Y1] ^ bit[Y_HI], bit[Z0] ^ bit[Z_HI], bit[Z1] ^ bit[Z_HI]])
    inner_moves = [functools.partial(flip, mask=move) for move in subsets((Y0, Y1, Z0, Z1))]

    far_early = flip(features[half // 2 :], full)
    top_moved = lax.switch(inner, inner_moves, top)
    top_later, top_moved = lax.optimization_barrier((top, top_moved))
    far_late = flip(top_later[: half // 2], full)
    bottom_moved = lax.switch(inner, inner_moves, far_early[half // 2 :])

    cross = bit[Y_HI]
    stays, crosses = jnp.where(cross, bottom_moved, top_moved), jnp.where(cross, top_moved, bottom_moved)
    along = (X0, X1, Z0 | Z1 | Z_HI)
    outer = packed([bit[place] ^ cross for place in (X0, X1, Z_HI)])
    rest = Y0 | Y1 | Y_HI | sum(along)
    outer_moves = [
        (lambda pair, move=move: (flip(pair[0], move ^ rest), flip(pair[1], move))) for move in subsets(along)
    ]
    crosses, stays = lax.switch(outer, outer_moves, (crosses, stays))

    sibling = jnp.where(swaps(mask), stays, crosses)
    swapped = flip(sibling, CORE)
    tiles = [("own", (features,)), ("flip", (far_late, far_early))]
    gradient = add_tiles(blocks, tiles, own_id, rounds, labels, features)
    tiles = [("pick", (swapped,))]
    return add_tiles(blocks, tiles, own_id, rounds, labels, features, gradient, (stays, crosses))


def solution(mesh):
    in_specs = (P(("gx", "gy"), None), P(), P())
    out_specs = P(("gx", "gy"), None)
    return jax.shard_map(
        on_device, mesh=mesh, in_specs=in_specs, out_specs=out_specs, check_vma=False
    )
```
